256 devices in a mesh: seq: 128 (over y, z, x_hi, core), head: 2 (over x_lo).
Axes of the slice: x: 4 (x_hi: 2, x_lo: 2; x = x_hi * 2 + x_lo), y: 4, z: 8, core: 2. Of those that a mesh axis runs over, the one named last changes fastest.
Arguments:
- queries: bfloat16 [32768, 2048], P(('seq', 'head')), may hold values from -28 to 28
- key_states: bfloat16 [32768, 512], P(('seq', 'head')), may hold values from -20 to 20
- value_vector_rows: bfloat16 [32768, 512], P(('seq', 'head')), may hold values from -6 to 6
- grad_output: bfloat16 [32768, 2048], P(('seq', 'head')), may hold values from -6 to 6
- doc_ids: int32 [256], replicated, may hold values from 0 to 31, never falling along the last dimension, each value on 1 to 64 neighbouring positions
- block_home: int32 [256], replicated, may hold values from 0 to 255, as said below
Outputs:
- attended: bfloat16 [32768, 2048], P('seq', 'head')
- grad_query: bfloat16 [32768, 2048], P('seq', 'head')
- key_gradient: bfloat16 [32768, 512], P('seq', 'head')
- value_gradient: bfloat16 [32768, 512], P('seq', 'head')
The draws below stay inside these ranges and needn't reach their ends.
Inputs may be any that keep to these rules, and one draw needn't show every extreme that they name: `block_home`: a permutation of the natural blocks; slots are numbered shard by shard, 2 slots to a seq shard; every block sits in its natural shard (block // 2) or one beside it, and across each boundary between neighbouring shards exactly one block moves each way.
All inputs are finite; a program needn't handle non-finite values.
Results may differ from the reference program's by a relative error of at most 0.025.
Values may be sent and summed in bfloat16 or wider, within the bound.
A program may use at most 192 MiB of HBM per device.

```python
import math
import jax
import jax.numpy as jnp
import numpy as np
from jax import lax

TOKENS_PER_PART = 256
BLK = 128
WINDOW = 2048
QUERY_HEADS = 16
KEY_VALUE_HEADS = 4
HEAD_SIZE = 128
CONTEXT_TOKENS = 32768
NBLOCKS = 256
N_SEQ = 128


def shared_base(key):
    gaussian_sample = jax.random.normal(jax.random.fold_in(key, 101), (CONTEXT_TOKENS, KEY_VALUE_HEADS * HEAD_SIZE), jnp.float32)
    return jnp.clip(gaussian_sample, -4.0, 4.0)


def draw_key_states(key, part):
    lowest_offset = shared_base(key)
    return lowest_offset.astype(jnp.bfloat16)


def draw_queries(key, part):
    own_draw = jnp.clip(jax.random.normal(jax.random.fold_in(key, 202), (CONTEXT_TOKENS, QUERY_HEADS * HEAD_SIZE), jnp.float32), -4.0, 4.0)
    return own_draw.astype(jnp.bfloat16)


def draw_block_home(key, part):
    block_count = TOKENS_PER_PART // BLK
    shard_total = NBLOCKS // block_count
    boundary = jnp.arange(shard_total, dtype=jnp.int32)
    flips = (boundary < shard_total - 1).astype(jnp.int32)
    earlier = jnp.concatenate([jnp.zeros((1,), jnp.int32), flips[:-1]])
    slot_index = jnp.arange(NBLOCKS, dtype=jnp.int32)
    shard_of = slot_index // block_count
    within = slot_index % block_count
    home = slot_index + jnp.where(within == block_count - 1, flips[shard_of], 0) - jnp.where(within == 0, earlier[shard_of], 0)
    turns = jax.random.randint(jax.random.fold_in(key, 12), (shard_total,), 0, block_count).astype(jnp.int32)
    source = shard_of * block_count + (within + turns[shard_of]) % block_count
    return home[source].astype(jnp.int32)


def block_scale(rng, dims, pieces, low, high):
    def one(dim, parts):
        heights = jax.random.uniform(jax.random.fold_in(jax.random.fold_in(rng, 6), dim), (parts,), jnp.float32, low / len(pieces), high / len(pieces))
        return jnp.repeat(jnp.exp(heights), dims[dim] // parts).reshape((-1,) + (1,) * (len(dims) - dim - 1))

    level = one(*pieces[0])
    for cut in pieces[1:]:
        level = level * one(*cut)
    return level


def profile(amount, total, bound, lean):
    weights = [(1 << 20) // math.isqrt(grade ** lean) + 1 for grade in range(2, amount + 1)]
    spare, counts = total - bound - (amount - 1), [1] * (amount - 1)
    while spare > 0:
        free = [i for i in range(amount - 1) if counts[i] < bound]
        whole, budget = sum([weights[i] for i in free]), spare
        for i in free:
            addition = min(bound - counts[i], max(1, budget * weights[i] // whole), spare)
            counts[i] = counts[i] + addition
            spare = spare - addition
    return np.array([bound] + counts)


def ragged(own_key, count, total, bound, slope):
    if count == 2:
        one = jax.random.randint(own_key, (), max(1, total - bound), min(bound, total - 1) + 1)
        return jnp.stack([one, total - one])
    sizes = jnp.asarray(profile(count, total, bound, slope), jnp.int32)
    twos = (count - 1) // 2
    source_of, receiver = sizes[1:1 + 2 * twos:2], sizes[2:2 + 2 * twos:2]
    room = jnp.minimum(source_of - 1, bound - receiver)
    passed = jax.random.randint(jax.random.fold_in(own_key, 1), (twos,), 0, 1 << 20) % (room + 1)
    sizes = sizes.at[1:1 + 2 * twos:2].set(source_of - passed).at[2:2 + 2 * twos:2].set(receiver + passed)
    return sizes[jax.random.permutation(jax.random.fold_in(own_key, 2), count)]


def noise(key, extent, spread, bound, cuts=(), held_as=jnp.bfloat16):
    array = spread * jax.random.normal(key, extent, jnp.float32)
    if cuts:
        array = array * block_scale(key, extent, cuts, -0.22, 0.18)
    return jnp.clip(array, -bound, bound).astype(held_as)


def setup_inputs(seed: int = 0) -> dict:
    seeds = jax.random.split(jax.random.key(seed), 7)
    queries = draw_queries(jax.random.fold_in(seeds[6], 71), 0)
    key_states = draw_key_states(jax.random.fold_in(seeds[6], 71), 0)
    value_vector_rows = noise(seeds[2], (CONTEXT_TOKENS, KEY_VALUE_HEADS * HEAD_SIZE), 1.0, 6.0, ((0, 256),))
    grad_output = noise(seeds[3], (CONTEXT_TOKENS, QUERY_HEADS * HEAD_SIZE), 1.0, 6.0, ((0, 256),))
    doc_ids = jnp.searchsorted(jnp.cumsum(ragged(seeds[4], NBLOCKS // 8, NBLOCKS, min(64, NBLOCKS // 2), 2)), jnp.arange(NBLOCKS), side="right").astype(jnp.int32)
    block_home = draw_block_home(jax.random.fold_in(seeds[6], 71), 0)
    return dict(queries=queries, key_states=key_states, value_vector_rows=value_vector_rows, grad_output=grad_output, doc_ids=doc_ids, block_home=block_home)


def reference(queries, key_states, value_vector_rows, grad_output, doc_ids, block_home):
    block_count = TOKENS_PER_PART // BLK
    reach = WINDOW // TOKENS_PER_PART
    queries_per_group = QUERY_HEADS // KEY_VALUE_HEADS
    reciprocal_root = 1.0 / math.sqrt(HEAD_SIZE)
    listing = jnp.arange(NBLOCKS, dtype=jnp.int32)
    inverse = jnp.zeros((NBLOCKS,), jnp.int32).at[block_home].set(listing)

    def natural(source):
        return source.reshape(NBLOCKS, BLK, source.shape[1])[inverse].reshape(CONTEXT_TOKENS, source.shape[1])
    query_natural_order = natural(queries)
    key_natural_order = natural(key_states)
    value_natural_order = natural(value_vector_rows)
    gradient_natural_order = natural(grad_output)
    filler_rows = reach * TOKENS_PER_PART
    reach_extent = filler_rows + TOKENS_PER_PART
    key_padded = jnp.concatenate([jnp.zeros((filler_rows, KEY_VALUE_HEADS * HEAD_SIZE), jnp.bfloat16), key_natural_order], axis=0)
    value_padded = jnp.concatenate([jnp.zeros((filler_rows, KEY_VALUE_HEADS * HEAD_SIZE), jnp.bfloat16), value_natural_order], axis=0)
    doc_tok = jnp.repeat(doc_ids, BLK)
    doc_pad = jnp.concatenate([jnp.full((filler_rows,), -1, jnp.int32), doc_tok])
    row_index = jnp.arange(TOKENS_PER_PART, dtype=jnp.int32)
    col_index = jnp.arange(reach_extent, dtype=jnp.int32)
    top_precision = lax.Precision.HIGHEST

    def shard_step(running_total, shard):
        begin_offset = (shard * TOKENS_PER_PART).astype(jnp.int32)
        local_query = lax.dynamic_slice_in_dim(query_natural_order, begin_offset, TOKENS_PER_PART, 0).reshape(TOKENS_PER_PART, KEY_VALUE_HEADS, queries_per_group, HEAD_SIZE).astype(jnp.float32)
        gradient_local = lax.dynamic_slice_in_dim(gradient_natural_order, begin_offset, TOKENS_PER_PART, 0).reshape(TOKENS_PER_PART, KEY_VALUE_HEADS, queries_per_group, HEAD_SIZE).astype(jnp.float32)
        local_keys = lax.dynamic_slice_in_dim(key_padded, begin_offset, reach_extent, 0).reshape(reach_extent, KEY_VALUE_HEADS, HEAD_SIZE).astype(jnp.float32)
        local_values = lax.dynamic_slice_in_dim(value_padded, begin_offset, reach_extent, 0).reshape(reach_extent, KEY_VALUE_HEADS, HEAD_SIZE).astype(jnp.float32)
        query_doc = lax.dynamic_slice_in_dim(doc_tok, begin_offset, TOKENS_PER_PART, 0)
        key_doc = lax.dynamic_slice_in_dim(doc_pad, begin_offset, reach_extent, 0)
        distance = row_index[:, None] + filler_rows - col_index[None, :]
        visible = (query_doc[:, None] == key_doc[None, :]) & (distance >= 0) & (distance < WINDOW)
        scores = jnp.einsum('tgqd,ugd->gqtu', local_query, local_keys, precision=top_precision) * reciprocal_root
        row_max = lax.optimization_barrier(jnp.max(jnp.where(visible, scores, -1e+30), axis=-1, keepdims=True))
        row_sum = lax.optimization_barrier(jnp.sum(jnp.where(visible, jnp.exp(scores - row_max), 0.0), axis=-1, keepdims=True))
        log_total = row_max + jnp.log(row_sum)
        prob = jnp.where(visible, jnp.exp(scores - log_total), 0.0)
        probability_lowered = lax.optimization_barrier(prob.astype(jnp.bfloat16)).astype(jnp.float32)
        attended = jnp.einsum('gqtu,ugd->tgqd', probability_lowered, local_values, precision=top_precision).astype(jnp.bfloat16)
        delta = jnp.transpose(lax.optimization_barrier(jnp.sum(gradient_local * attended.astype(jnp.float32), axis=-1)), (1, 2, 0))
        grad_prob = jnp.einsum('tgqd,ugd->gqtu', gradient_local, local_values, precision=top_precision)
        score_gradient = lax.optimization_barrier((prob * (grad_prob - delta[..., None])).astype(jnp.bfloat16)).astype(jnp.float32)
        grad_query = (jnp.einsum('gqtu,ugd->tgqd', score_gradient, local_keys, precision=top_precision) * reciprocal_root).astype(jnp.bfloat16)
        key_contribution = jnp.einsum('nzev,enzx->vnx', score_gradient, local_query, precision=top_precision).reshape(reach_extent, KEY_VALUE_HEADS * HEAD_SIZE)
        value_contribution = jnp.einsum('nzev,enzx->vnx', probability_lowered, gradient_local, precision=top_precision).reshape(reach_extent, KEY_VALUE_HEADS * HEAD_SIZE)
        shard_term = jnp.concatenate([key_contribution, value_contribution], axis=1)
        old = lax.dynamic_slice_in_dim(running_total, begin_offset, reach_extent, 0)
        running_total = lax.dynamic_update_slice_in_dim(running_total, old + shard_term, begin_offset, 0)
        return (running_total, (attended.reshape(TOKENS_PER_PART, QUERY_HEADS * HEAD_SIZE), grad_query.reshape(TOKENS_PER_PART, QUERY_HEADS * HEAD_SIZE)))
    running_begin = jnp.zeros((filler_rows + CONTEXT_TOKENS, 2 * KEY_VALUE_HEADS * HEAD_SIZE), jnp.float32)
    running_total, stacked = lax.scan(shard_step, running_begin, jnp.arange(N_SEQ, dtype=jnp.int32))
    attended_all = stacked[0].reshape(CONTEXT_TOKENS, QUERY_HEADS * HEAD_SIZE)
    grad_query_all = stacked[1].reshape(CONTEXT_TOKENS, QUERY_HEADS * HEAD_SIZE)
    key_gradient = (running_total[filler_rows:, :KEY_VALUE_HEADS * HEAD_SIZE] * reciprocal_root).astype(jnp.bfloat16)
    value_gradient = running_total[filler_rows:, KEY_VALUE_HEADS * HEAD_SIZE:].astype(jnp.bfloat16)
    return (attended_all, grad_query_all, key_gradient, value_gradient)
```

```python
import math

import jax
import jax.numpy as jnp
from jax import lax
from jax.experimental import pallas as pl
from jax.experimental.pallas import tpu as pltpu
from jax.sharding import PartitionSpec as P

BLK = 128
HEAD = 128
TOK = 256
QH = 8
KVH = 2
PER = 4
QW = QH * HEAD
KW = KVH * HEAD
NSEQ = 128
ND = 9
WIDE = PER * TOK
SCALE = 1.0 / math.sqrt(HEAD)
C2 = SCALE * math.log2(math.e)
LOW = -1e30
MESH = pl.DeviceIdType.MESH
F32 = jnp.float32
BF16 = jnp.bfloat16


def dot(a, b):
    return lax.dot_general(a, b, (((1,), (0,)), ((), ())), preferred_element_type=F32)


def dot_nt(a, b):
    return lax.dot_general(a, b, (((1,), (1,)), ((), ())), preferred_element_type=F32)


def flip(a):
    return jnp.transpose(a, (1, 0))


def kernel(
    doc_ref,
    home_ref,
    q_in,
    k_in,
    v_in,
    g_in,
    att_ref,
    dq_ref,
    dk_ref,
    dv_ref,
    rq,
    rk,
    rv,
    rg,
    kv,
    kvt,
    qs,
    gs,
    gst,
    s_buf,
    p_buf,
    ds_buf,
    mx,
    lsum,
    delta,
    ot,
    attt,
    dqt,
    acc,
    sb,
    rr4,
    rr3,
    rr2,
    rr1,
    own_send,
    own_recv,
    halo_send,
    halo_recv,
    back_send,
    back_recv,
):
    s = lax.axis_index("seq")
    h = lax.axis_index("head")
    core = lax.rem(s, 2)
    xhi = lax.rem(lax.div(s, 2), 2)
    first = s == 0
    last = s == NSEQ - 1
    up4 = lax.rem(s + 4, NSEQ)
    down4 = lax.rem(s + NSEQ - 4, NSEQ)
    part_x = s + 2 - 4 * xhi
    part_c = s + 1 - 2 * core
    right = jnp.minimum(s + 1, NSEQ - 1)
    left = jnp.maximum(s - 1, 0)

    barrier = pltpu.get_barrier_semaphore()

    def greet(seq, head):
        pl.semaphore_signal(barrier, inc=1, device_id=(seq, head), device_id_type=MESH)

    for side in (left, right):
        greet(side, 1 - h)

        @pl.when(side != s)
        def _():
            greet(side, h)

    for other in (up4, down4, part_x):
        greet(other, h)
    edge = jnp.where(first | last, 1, 0)
    pl.semaphore_wait(barrier, 7 - edge)

    ins = (k_in, v_in, q_in, g_in)
    slots = (rk, rv, rq, rg)
    widths = (KW, KW, QW, QW)

    def direct(arrays, what):
        for side, seq in ((0, right), (1, left)):
            at_end = last if side == 0 else first
            base = jnp.where(at_end, 2 * (1 - side), 2 * side)
            slot = base + h
            for head in range(2):
                mine = at_end & (h == head)
                for a in arrays:
                    src = ins[a].at[:, pl.ds(head * widths[a], widths[a])]
                    copy = pltpu.make_async_remote_copy(
                        src_ref=src,
                        dst_ref=slots[a].at[slot],
                        send_sem=own_send.at[a, side, head],
                        recv_sem=own_recv.at[a, slot],
                        device_id=(seq, head),
                        device_id_type=MESH,
                    )
                    local = pltpu.make_async_copy(src, slots[a].at[slot], own_recv.at[a, slot])

                    if what == "start":

                        @pl.when(jnp.logical_not(mine))
                        def _():
                            copy.start()

                        @pl.when(mine)
                        def _():
                            local.start()

                    else:

                        @pl.when(jnp.logical_not(mine))
                        def _():
                            copy.wait_send()

    def landed(arrays):
        for a in arrays:
            for i in range(4):
                pltpu.make_async_copy(
                    slots[a].at[i], slots[a].at[i], own_recv.at[a, i]
                ).wait()

    direct((0, 1), "start")

    picks = []
    for p in range(2):
        wanted = 2 * s + p
        pick = jnp.int32(0)
        for i in range(4):
            shard = left if i < 2 else right
            pick = jnp.where(home_ref[2 * shard + i % 2] == wanted, i, pick)
        picks.append(pick)

    acc[...] = jnp.zeros_like(acc)
    ot[...] = jnp.zeros_like(ot)
    dqt[...] = jnp.zeros_like(dqt)
    mx[...] = jnp.full_like(mx, LOW)

    landed((0, 1))
    for p in range(2):
        for g in range(KVH):
            rows = pl.ds(p * BLK, BLK)
            cols = pl.ds(g * HEAD, HEAD)
            kv[0, g, rows, :] = rk[picks[p], :, cols]
            kv[0, KVH + g, rows, :] = rv[picks[p], :, cols]

    def halo(src, dst, seq, sem):
        return pltpu.make_async_remote_copy(
            src_ref=kv.at[src],
            dst_ref=kv.at[dst],
            send_sem=halo_send.at[sem],
            recv_sem=halo_recv.at[dst],
            device_id=(seq, h),
            device_id_type=MESH,
        )

    def have(d):
        pltpu.make_async_copy(kv.at[d], kv.at[d], halo_recv.at[d]).wait()

    z0 = halo(0, 4, up4, 0)
    z4 = halo(4, 8, up4, 1)
    x0 = halo(0, 2, part_x, 2)
    x4 = halo(4, 6 - 4 * xhi, part_x, 3)
    x8 = halo(8, 6, part_x, 4)
    c0 = halo(0, 1, part_c, 5)
    c2 = halo(2, 3 - 2 * core, part_c, 6)
    c4 = halo(4, 5 - 2 * core, part_c, 7)
    c6 = halo(6, 7 - 2 * core, part_c, 8)
    c8 = halo(8, 7, part_c, 9)

    z0.start()

    @pl.when(xhi == 0)
    def _():
        x0.start()

    @pl.when(core == 0)
    def _():
        c0.start()

    direct((2, 3), "start")

    have(4)
    z4.start()
    x4.start()
    c4.start()
    have(8)

    @pl.when(xhi == 1)
    def _():
        x8.start()

    @pl.when(core == 1)
    def _():
        c8.start()

    have(2)
    c2.start()
    have(6)
    c6.start()
    for d in (1, 3, 5, 7):
        have(d)

    def turn(d, carry):
        for i in range(2 * KVH):
            kvt[i, d] = flip(kv[d, i])
        return carry

    lax.fori_loop(0, ND, turn, 0)

    landed((2,))
    for p in range(2):
        for i in range(QH):
            rows = pl.ds((i % PER) * TOK + p * BLK, BLK)
            qs[i // PER, rows, :] = rq[picks[p], :, pl.ds(i * HEAD, HEAD)]

    lane = lax.broadcasted_iota(jnp.int32, (1, TOK), 1)

    def hidden(d, pu):
        back = s - d
        key_doc = doc_ref[jnp.maximum(2 * back + pu, 0)]
        low = []
        for pt in range(2):
            seen = (doc_ref[2 * s + pt] == key_doc) & (back >= 0)
            low.append(jnp.where(seen, 0.0, LOW).astype(F32))
        return jnp.where(lane < BLK, low[0], low[1])

    def score(d, g, shape):
        for j in range(PER):
            cols = pl.ds(j * TOK, TOK)
            tile = dot_nt(kv[d, g], qs[g, cols, :])
            if shape is not None:
                row = lax.broadcasted_iota(jnp.int32, (TOK, TOK), 0)
                col = lax.broadcasted_iota(jnp.int32, (TOK, TOK), 1)
                keep = row <= col if shape == "own" else row > col
                tile = jnp.where(keep, tile, LOW)
            s_buf[g * ND + d, :, cols] = tile
            best = mx[g, :, cols]
            for pu in range(2):
                top = jnp.max(tile[pu * BLK : (pu + 1) * BLK].reshape(BLK // 8, 8, TOK), axis=0)
                best = jnp.maximum(best, top + hidden(d, pu))
            mx[g, :, cols] = best

    for d, shape in ((0, "own"), (8, "far")):
        for g in range(KVH):
            score(d, g, shape)

    def score_step(i, carry):
        score(1 + lax.div(i, KVH), lax.rem(i, KVH), None)
        return carry

    lax.fori_loop(0, (ND - 2) * KVH, score_step, 0)

    def weigh(g, carry):
        lsum[...] = jnp.zeros_like(lsum)
        top = jnp.max(mx[g], axis=0, keepdims=True) * C2

        def step(d, inner):
            low = [hidden(d, pu) for pu in range(2)]
            for j in range(PER):
                cols = pl.ds(j * TOK, TOK)
                total = lsum[:, cols]
                for pu in range(2):
                    rows = pl.ds(pu * BLK, BLK)
                    base = top[:, j * TOK : (j + 1) * TOK] - low[pu]
                    e = jnp.exp2(s_buf[g * ND + d, rows, cols] * C2 - base)
                    total = total + jnp.sum(e.reshape(BLK // 8, 8, TOK), axis=0)
                    p_buf[g * ND + d, rows, cols] = e.astype(BF16)
                lsum[:, cols] = total
                ot[g, :, cols] += dot(kvt[KVH + g, d], p_buf[g * ND + d, :, cols])
            return inner

        lax.fori_loop(0, ND, step, 0)
        inv = 1.0 / jnp.sum(lsum[...], axis=0, keepdims=True)
        attt[g] = (ot[g] * inv).astype(BF16)
        delta[g] = inv
        return carry

    lax.fori_loop(0, KVH, weigh, 0)

    landed((3,))
    for i in range(QH):
        g, j = i // PER, i % PER
        cols = pl.ds(j * TOK, TOK)
        for p in range(2):
            gs[g, pl.ds(j * TOK + p * BLK, BLK), :] = rg[picks[p], :, pl.ds(i * HEAD, HEAD)]
        low = (flip(gs[g, cols, :]).astype(F32) * delta[g, :, cols]).astype(BF16)
        gst[g, :, cols] = low
        gs[g, cols, :] = flip(low)
        a = attt[g, :, cols]
        delta[g, :, cols] = jnp.sum(low.astype(F32) * a.astype(F32), axis=0, keepdims=True)
        att_ref[:, pl.ds(i * HEAD, HEAD)] = flip(a)

    def slope(d):
        def one(g, carry):
            for j in range(PER):
                cols = pl.ds(j * TOK, TOK)
                dp = dot(kv[d, KVH + g], gst[g, :, cols])
                e = p_buf[g * ND + d, :, cols].astype(F32)
                ds_buf[:, cols] = (e * (dp - delta[g, :, cols])).astype(BF16)
                dqt[g, :, cols] += dot(kvt[g, d], ds_buf[:, cols])
            acc[d, g] += dot(ds_buf[...], qs[g])
            acc[d, KVH + g] += dot(p_buf[g * ND + d], gs[g])
            return carry

        lax.fori_loop(0, KVH, one, 0)

    def give(d, dst, seq, sem):
        return pltpu.make_async_remote_copy(
            src_ref=sb.at[d],
            dst_ref=dst,
            send_sem=back_send.at[sem],
            recv_sem=back_recv.at[sem],
            device_id=(seq, h),
            device_id_type=MESH,
        )

    b7 = give(7, rr4.at[3], part_c, 3)
    b5 = give(5, rr4.at[2], part_c, 2)
    b3 = give(3, rr4.at[1], part_c, 1)
    b1 = give(1, rr4.at[0], part_c, 0)
    b6 = give(6, rr3.at[1], part_x, 5)
    b2 = give(2, rr3.at[0], part_x, 4)
    b8 = give(8, rr2, down4, 6)
    b4 = give(4, rr1, down4, 7)

    def post(d, copy):
        sb[d] = acc[d].astype(BF16)
        copy.start()

    def take(copy, ref, d):
        copy.wait_recv()
        acc[d] += ref[...].astype(F32)

    slope(7)
    post(7, b7)
    slope(5)
    post(5, b5)
    slope(6)
    take(b7, rr4.at[3], 6 + 2 * core)
    take(b5, rr4.at[2], 4 + 2 * core)
    post(6, b6)
    slope(3)
    post(3, b3)
    slope(1)
    post(1, b1)
    slope(8)
    take(b6, rr3.at[1], 4 + 4 * xhi)
    post(8, b8)
    slope(2)
    take(b3, rr4.at[1], 2 + 2 * core)
    take(b1, rr4.at[0], 2 * core)
    post(2, b2)
    slope(4)
    take(b2, rr3.at[0], 4 * xhi)
    take(b8, rr2, 4)
    post(4, b4)
    slope(0)
    for i in range(QH):
        g, j = i // PER, i % PER
        low = (dqt[g, :, pl.ds(j * TOK, TOK)] * SCALE).astype(BF16)
        dq_ref[:, pl.ds(i * HEAD, HEAD)] = flip(low)
    take(b4, rr1, 0)
    for g in range(KVH):
        dk_ref[:, pl.ds(g * HEAD, HEAD)] = (acc[0, g] * SCALE).astype(BF16)
        dv_ref[:, pl.ds(g * HEAD, HEAD)] = acc[0, KVH + g].astype(BF16)

    direct((0, 1, 2, 3), "wait")
    for copy in (z0, z4, x4, c2, c4, c6, b7, b5, b3, b1, b6, b2, b8, b4):
        copy.wait_send()

    @pl.when(xhi == 0)
    def _():
        x0.wait_send()

    @pl.when(xhi == 1)
    def _():
        x8.wait_send()

    @pl.when(core == 0)
    def _():
        c0.wait_send()

    @pl.when(core == 1)
    def _():
        c8.wait_send()


def per_device(queries, key_states, value_vector_rows, grad_output, doc_ids, block_home):
    vmem = pl.BlockSpec(memory_space=pltpu.VMEM)
    smem = pl.BlockSpec(memory_space=pltpu.SMEM)
    anywhere = pl.BlockSpec(memory_space=pl.ANY)
    out = pl.pallas_call(
        kernel,
        out_shape=(
            jax.ShapeDtypeStruct((TOK, QW), BF16),
            jax.ShapeDtypeStruct((TOK, QW), BF16),
            jax.ShapeDtypeStruct((TOK, KW), BF16),
            jax.ShapeDtypeStruct((TOK, KW), BF16),
        ),
        in_specs=[smem, smem, anywhere, anywhere, anywhere, anywhere],
        out_specs=(vmem, vmem, vmem, vmem),
        scratch_shapes=[
            pltpu.VMEM((4, BLK, QW), BF16),
            pltpu.VMEM((4, BLK, KW), BF16),
            pltpu.VMEM((4, BLK, KW), BF16),
            pltpu.VMEM((4, BLK, QW), BF16),
            pltpu.VMEM((ND, 2 * KVH, TOK, HEAD), BF16),
            pltpu.VMEM((2 * KVH, ND, HEAD, TOK), BF16),
            pltpu.VMEM((KVH, WIDE, HEAD), BF16),
            pltpu.VMEM((KVH, WIDE, HEAD), BF16),
            pltpu.VMEM((KVH, HEAD, WIDE), BF16),
            pltpu.VMEM((KVH * ND, TOK, WIDE), F32),
            pltpu.VMEM((KVH * ND, TOK, WIDE), BF16),
            pltpu.VMEM((TOK, WIDE), BF16),
            pltpu.VMEM((KVH, 8, WIDE), F32),
            pltpu.VMEM((8, WIDE), F32),
            pltpu.VMEM((KVH, 1, WIDE), F32),
            pltpu.VMEM((KVH, HEAD, WIDE), F32),
            pltpu.VMEM((KVH, HEAD, WIDE), BF16),
            pltpu.VMEM((KVH, HEAD, WIDE), F32),
            pltpu.VMEM((ND, 2 * KVH, TOK, HEAD), F32),
            pltpu.VMEM((ND, 2 * KVH, TOK, HEAD), BF16),
            pltpu.VMEM((4, 2 * KVH, TOK, HEAD), BF16),
            pltpu.VMEM((2, 2 * KVH, TOK, HEAD), BF16),
            pltpu.VMEM((2 * KVH, TOK, HEAD), BF16),
            pltpu.VMEM((2 * KVH, TOK, HEAD), BF16),
            pltpu.SemaphoreType.DMA((4, 2, 2)),
            pltpu.SemaphoreType.DMA((4, 4)),
            pltpu.SemaphoreType.DMA((10,)),
            pltpu.SemaphoreType.DMA((ND,)),
            pltpu.SemaphoreType.DMA((8,)),
            pltpu.SemaphoreType.DMA((8,)),
        ],
        compiler_params=pltpu.CompilerParams(
            collective_id=0,
            has_side_effects=True,
            vmem_limit_bytes=60 * 1024 * 1024,
        ),
        cost_estimate=pl.CostEstimate(
            flops=8 * 10**9, bytes_accessed=3 * 10**6, transcendentals=5 * 10**6
        ),
    )(doc_ids, block_home, queries, key_states, value_vector_rows, grad_output)
    return out


def solution(mesh):
    return jax.shard_map(
        per_device,
        mesh=mesh,
        in_specs=(
            P(("seq", "head"), None),
            P(("seq", "head"), None),
            P(("seq", "head"), None),
            P(("seq", "head"), None),
            P(),
            P(),
        ),
        out_specs=(P("seq", "head"), P("seq", "head"), P("seq", "head"), P("seq", "head")),
        check_vma=False,
    )
```

```python
import math

import jax
import jax.numpy as jnp
from jax import lax
from jax.experimental import pallas as pl
from jax.experimental.pallas import tpu as pltpu
from jax.sharding import PartitionSpec as P

BLK = 128
HEAD = 128
TOK = 256
QH = 8
KVH = 2
PER = 4
QW = QH * HEAD
KW = KVH * HEAD
NSEQ = 128
ND = 9
WIDE = PER * TOK
SCALE = 1.0 / math.sqrt(HEAD)
C2 = SCALE * math.log2(math.e)
LOW = -1e30
MESH = pl.DeviceIdType.MESH
F32 = jnp.float32
BF16 = jnp.bfloat16


def dot(a, b):
    return lax.dot_general(a, b, (((1,), (0,)), ((), ())), preferred_element_type=F32)


def dot_nt(a, b):
    return lax.dot_general(a, b, (((1,), (1,)), ((), ())), preferred_element_type=F32)


def flip(a):
    return jnp.transpose(a, (1, 0))


def kernel(
    doc_ref,
    home_ref,
    q_in,
    k_in,
    v_in,
    g_in,
    att_ref,
    dq_ref,
    dk_ref,
    dv_ref,
    loc_q,
    loc_k,
    loc_v,
    loc_g,
    m_out,
    m_got,
    x_out,
    x_got,
    c_out,
    c_got,
    kv,
    kvt,
    qs,
    gs,
    gst,
    s_buf,
    p_buf,
    ds_buf,
    mx,
    lsum,
    delta,
    ot,
    attt,
    dqt,
    acc,
    sb,
    rr4,
    rr3,
    rr2,
    rr1,
    load_sem,
    move_send,
    move_recv,
    halo_send,
    halo_recv,
    back_send,
    back_recv,
):
    s = lax.axis_index("seq")
    h = lax.axis_index("head")
    core = lax.rem(s, 2)
    xhi = lax.rem(lax.div(s, 2), 2)
    up4 = lax.rem(s + 4, NSEQ)
    down4 = lax.rem(s + NSEQ - 4, NSEQ)
    part_x = s + 2 - 4 * xhi
    part_c = s + 1 - 2 * core
    cross = jnp.clip(s - 1 + 2 * core, 0, NSEQ - 1)

    ins = (k_in, v_in, q_in, g_in)
    locs = (loc_k, loc_v, loc_q, loc_g)
    widths = (KW, KW, QW, QW)

    def load(a, half):
        return pltpu.make_async_copy(
            ins[a].at[:, pl.ds(half * widths[a], widths[a])],
            locs[a].at[half],
            load_sem.at[a, half],
        )

    for a in range(4):
        for half in range(2):
            load(a, half).start()

    barrier = pltpu.get_barrier_semaphore()

    def greet(seq, head):
        pl.semaphore_signal(barrier, inc=1, device_id=(seq, head), device_id_type=MESH)

    greet(s, 1 - h)
    greet(cross, 1 - h)
    for other in (part_c, part_x, up4, down4):
        greet(other, h)
    pl.semaphore_wait(barrier, 6)

    crosses = lax.div(home_ref[2 * s + h], 2) != part_c
    told = jnp.where(crosses, h, 1 - h)

    def column(i):
        if i < 2 * KVH:
            return i % 2, i // 2
        i -= 2 * KVH
        return 2 + i // QH, i % QH

    pieces = ((0, 2), (2, 4), (4, 8), (8, 12), (12, 16), (16, 20))

    def own(i, half):
        a, c = column(i)
        return locs[a][half, :, pl.ds(c * HEAD, HEAD)]

    def move(way, piece):
        lo, hi = pieces[piece]
        src, dst, to = (
            (m_out, m_got, (s, 1 - h)),
            (x_out, x_got, (cross, 1 - h)),
            (c_out, c_got, (part_c, h)),
        )[way]
        return pltpu.make_async_remote_copy(
            src_ref=src.at[pl.ds(lo, hi - lo)],
            dst_ref=dst.at[pl.ds(lo, hi - lo)],
            send_sem=move_send.at[way, piece],
            recv_sem=move_recv.at[way, piece],
            device_id=to,
            device_id_type=MESH,
        )

    def tell(piece):
        for i in range(*pieces[piece]):
            m_out[i] = own(i, told)
        move(0, piece).start()

    def pass_on(piece):
        move(0, piece).wait_recv()
        for i in range(*pieces[piece]):
            got = m_got[i]
            x_out[i] = lax.select(crosses, own(i, 1 - h), got)
            c_out[i] = lax.select(crosses, got, own(i, h))
        move(1, piece).start()
        move(2, piece).start()

    inside = []
    for p in range(2):
        want = 2 * s + p
        inside.append((home_ref[2 * part_c] == want) | (home_ref[2 * part_c + 1] == want))

    def settle(piece):
        move(1, piece).wait_recv()
        move(2, piece).wait_recv()
        for i in range(*pieces[piece]):
            a, c = column(i)
            for p in range(2):
                block = lax.select(inside[p], c_got[i], x_got[i])
                if a < 2:
                    kv[0, c, a, pl.ds(p * BLK, BLK), :] = block
                else:
                    rows = pl.ds((c % PER) * TOK + p * BLK, BLK)
                    (qs if a == 2 else gs)[c // PER, rows, :] = block

    def halo(src, dst, seq, sem, g):
        return pltpu.make_async_remote_copy(
            src_ref=kv.at[src, g],
            dst_ref=kv.at[dst, g],
            send_sem=halo_send.at[sem, g],
            recv_sem=halo_recv.at[dst, g],
            device_id=(seq, h),
            device_id_type=MESH,
        )

    def have(d, g):
        pltpu.make_async_copy(kv.at[d, g], kv.at[d, g], halo_recv.at[d, g]).wait()

    z0, z4, x0, x4, x8, c0, c2, c4, c6, c8 = (
        [halo(src, dst, seq, sem, g) for g in range(KVH)]
        for sem, (src, dst, seq) in enumerate(
            (
                (0, 4, up4),
                (4, 8, up4),
                (0, 2, part_x),
                (4, 6 - 4 * xhi, part_x),
                (8, 6, part_x),
                (0, 1, part_c),
                (2, 3 - 2 * core, part_c),
                (4, 5 - 2 * core, part_c),
                (6, 7 - 2 * core, part_c),
                (8, 7, part_c),
            )
        )
    )

    for a in (0, 1):
        for half in range(2):
            load(a, half).wait()
    tell(0)
    tell(1)
    acc[...] = jnp.zeros_like(acc)
    pass_on(0)
    pass_on(1)
    for a in (2, 3):
        for half in range(2):
            load(a, half).wait()
    tell(2)
    tell(3)
    ot[...] = jnp.zeros_like(ot)
    dqt[...] = jnp.zeros_like(dqt)
    mx[...] = jnp.full_like(mx, LOW)
    for g in range(KVH):
        settle(g)
        z0[g].start()

        @pl.when(xhi == 0)
        def _():
            x0[g].start()

        @pl.when(core == 0)
        def _():
            c0[g].start()

    tell(4)
    tell(5)
    pass_on(2)
    pass_on(3)
    for g in range(KVH):
        have(4, g)
        z4[g].start()
        x4[g].start()
        c4[g].start()
    pass_on(4)
    pass_on(5)
    for g in range(KVH):
        have(8, g)

        @pl.when(xhi == 1)
        def _():
            x8[g].start()

        @pl.when(core == 1)
        def _():
            c8[g].start()

    for d, copy in ((2, c2), (6, c6)):
        for g in range(KVH):
            have(d, g)
            copy[g].start()
    for d in (1, 3, 5, 7):
        for g in range(KVH):
            have(d, g)

    def turn(d, carry):
        for g in range(KVH):
            for kind in range(2):
                kvt[kind * KVH + g, d] = flip(kv[d, g, kind])
        return carry

    lax.fori_loop(0, ND, turn, 0)

    settle(2)
    settle(3)

    lane = lax.broadcasted_iota(jnp.int32, (1, TOK), 1)

    def hidden(d, pu):
        back = s - d
        key_doc = doc_ref[jnp.maximum(2 * back + pu, 0)]
        low = []
        for pt in range(2):
            seen = (doc_ref[2 * s + pt] == key_doc) & (back >= 0)
            low.append(jnp.where(seen, 0.0, LOW).astype(F32))
        return jnp.where(lane < BLK, low[0], low[1])

    def score(d, g, shape):
        for j in range(PER):
            cols = pl.ds(j * TOK, TOK)
            tile = dot_nt(kv[d, g, 0], qs[g, cols, :])
            if shape is not None:
                row = lax.broadcasted_iota(jnp.int32, (TOK, TOK), 0)
                col = lax.broadcasted_iota(jnp.int32, (TOK, TOK), 1)
                keep = row <= col if shape == "own" else row > col
                tile = jnp.where(keep, tile, LOW)
            s_buf[g * ND + d, :, cols] = tile
            best = mx[g, :, cols]
            for pu in range(2):
                top = jnp.max(tile[pu * BLK : (pu + 1) * BLK].reshape(BLK // 8, 8, TOK), axis=0)
                best = jnp.maximum(best, top + hidden(d, pu))
            mx[g, :, cols] = best

    for d, shape in ((0, "own"), (8, "far")):
        for g in range(KVH):
            score(d, g, shape)

    def score_step(i, carry):
        score(1 + lax.div(i, KVH), lax.rem(i, KVH), None)
        return carry

    lax.fori_loop(0, (ND - 2) * KVH, score_step, 0)

    def weigh(g, carry):
        lsum[...] = jnp.zeros_like(lsum)
        top = jnp.max(mx[g], axis=0, keepdims=True) * C2

        def step(d, inner):
            low = [hidden(d, pu) for pu in range(2)]
            for j in range(PER):
                cols = pl.ds(j * TOK, TOK)
                total = lsum[:, cols]
                for pu in range(2):
                    rows = pl.ds(pu * BLK, BLK)
                    base = top[:, j * TOK : (j + 1) * TOK] - low[pu]
                    e = jnp.exp2(s_buf[g * ND + d, rows, cols] * C2 - base)
                    total = total + jnp.sum(e.reshape(BLK // 8, 8, TOK), axis=0)
                    p_buf[g * ND + d, rows, cols] = e.astype(BF16)
                lsum[:, cols] = total
                ot[g, :, cols] += dot(kvt[KVH + g, d], p_buf[g * ND + d, :, cols])
            return inner

        lax.fori_loop(0, ND, step, 0)
        inv = 1.0 / jnp.sum(lsum[...], axis=0, keepdims=True)
        attt[g] = (ot[g] * inv).astype(BF16)
        delta[g] = inv
        return carry

    lax.fori_loop(0, KVH, weigh, 0)

    settle(4)
    settle(5)
    for i in range(QH):
        g, j = i // PER, i % PER
        cols = pl.ds(j * TOK, TOK)
        low = (flip(gs[g, cols, :]).astype(F32) * delta[g, :, cols]).astype(BF16)
        gst[g, :, cols] = low
        gs[g, cols, :] = flip(low)
        a = attt[g, :, cols]
        delta[g, :, cols] = jnp.sum(low.astype(F32) * a.astype(F32), axis=0, keepdims=True)
        att_ref[:, pl.ds(i * HEAD, HEAD)] = flip(a)

    def slope(d, g):
        for j in range(PER):
            cols = pl.ds(j * TOK, TOK)
            dp = dot(kv[d, g, 1], gst[g, :, cols])
            e = p_buf[g * ND + d, :, cols].astype(F32)
            ds_buf[:, cols] = (e * (dp - delta[g, :, cols])).astype(BF16)
            dqt[g, :, cols] += dot(kvt[g, d], ds_buf[:, cols])
        acc[d, g, 0] += dot(ds_buf[...], qs[g])
        acc[d, g, 1] += dot(p_buf[g * ND + d], gs[g])

    def give(d, dst, seq, sem):
        return [
            pltpu.make_async_remote_copy(
                src_ref=sb.at[d, g],
                dst_ref=dst.at[g],
                send_sem=back_send.at[sem, g],
                recv_sem=back_recv.at[sem, g],
                device_id=(seq, h),
                device_id_type=MESH,
            )
            for g in range(KVH)
        ]

    b7 = give(7, rr4.at[3], part_c, 3)
    b5 = give(5, rr4.at[2], part_c, 2)
    b3 = give(3, rr4.at[1], part_c, 1)
    b1 = give(1, rr4.at[0], part_c, 0)
    b6 = give(6, rr3.at[1], part_x, 5)
    b2 = give(2, rr3.at[0], part_x, 4)
    b8 = give(8, rr2, down4, 6)
    b4 = give(4, rr1, down4, 7)

    def post(d, copy, g):
        sb[d, g] = acc[d, g].astype(BF16)
        copy[g].start()

    def take(copy, ref, d, g):
        copy[g].wait_recv()
        acc[d, g] += ref[g].astype(F32)

    for g in range(KVH):
        slope(7, g)
        post(7, b7, g)
        slope(5, g)
        post(5, b5, g)
        slope(6, g)
        take(b7, rr4.at[3], 6 + 2 * core, g)
        take(b5, rr4.at[2], 4 + 2 * core, g)
        post(6, b6, g)
    for g in range(KVH):
        slope(3, g)
        post(3, b3, g)
        slope(1, g)
        post(1, b1, g)
        slope(2, g)
        take(b3, rr4.at[1], 2 + 2 * core, g)
        take(b1, rr4.at[0], 2 * core, g)
        post(2, b2, g)
        slope(8, g)
        take(b6, rr3.at[1], 4 + 4 * xhi, g)
        post(8, b8, g)
    for g in range(KVH):
        slope(4, g)
        slope(0, g)
        take(b2, rr3.at[0], 4 * xhi, g)
        take(b8, rr2, 4, g)
        post(4, b4, g)
    for i in range(QH):
        g, j = i // PER, i % PER
        low = (dqt[g, :, pl.ds(j * TOK, TOK)] * SCALE).astype(BF16)
        dq_ref[:, pl.ds(i * HEAD, HEAD)] = flip(low)
    for g in range(KVH):
        take(b4, rr1, 0, g)
        dk_ref[:, pl.ds(g * HEAD, HEAD)] = (acc[0, g, 0] * SCALE).astype(BF16)
        dv_ref[:, pl.ds(g * HEAD, HEAD)] = acc[0, g, 1].astype(BF16)

    for way in range(3):
        for piece in range(len(pieces)):
            move(way, piece).wait_send()
    for copy in (z0, z4, x4, c2, c4, c6, b7, b5, b3, b1, b6, b2, b8, b4):
        for g in range(KVH):
            copy[g].wait_send()

    for ahead, copy in ((xhi == 0, x0), (xhi == 1, x8), (core == 0, c0), (core == 1, c8)):

        @pl.when(ahead)
        def _():
            for g in range(KVH):
                copy[g].wait_send()


def per_device(queries, key_states, value_vector_rows, grad_output, doc_ids, block_home):
    vmem = pl.BlockSpec(memory_space=pltpu.VMEM)
    smem = pl.BlockSpec(memory_space=pltpu.SMEM)
    anywhere = pl.BlockSpec(memory_space=pl.ANY)
    out = pl.pallas_call(
        kernel,
        out_shape=(
            jax.ShapeDtypeStruct((TOK, QW), BF16),
            jax.ShapeDtypeStruct((TOK, QW), BF16),
            jax.ShapeDtypeStruct((TOK, KW), BF16),
            jax.ShapeDtypeStruct((TOK, KW), BF16),
        ),
        in_specs=[smem, smem, anywhere, anywhere, anywhere, anywhere],
        out_specs=(vmem, vmem, vmem, vmem),
        scratch_shapes=[
            pltpu.VMEM((2, BLK, QW), BF16),
            pltpu.VMEM((2, BLK, KW), BF16),
            pltpu.VMEM((2, BLK, KW), BF16),
            pltpu.VMEM((2, BLK, QW), BF16),
            *[pltpu.VMEM((2 * KVH + 2 * QH, BLK, HEAD), BF16) for _ in range(6)],
            pltpu.VMEM((ND, KVH, 2, TOK, HEAD), BF16),
            pltpu.VMEM((2 * KVH, ND, HEAD, TOK), BF16),
            pltpu.VMEM((KVH, WIDE, HEAD), BF16),
            pltpu.VMEM((KVH, WIDE, HEAD), BF16),
            pltpu.VMEM((KVH, HEAD, WIDE), BF16),
            pltpu.VMEM((KVH * ND, TOK, WIDE), F32),
            pltpu.VMEM((KVH * ND, TOK, WIDE), BF16),
            pltpu.VMEM((TOK, WIDE), BF16),
            pltpu.VMEM((KVH, 8, WIDE), F32),
            pltpu.VMEM((8, WIDE), F32),
            pltpu.VMEM((KVH, 1, WIDE), F32),
            pltpu.VMEM((KVH, HEAD, WIDE), F32),
            pltpu.VMEM((KVH, HEAD, WIDE), BF16),
            pltpu.VMEM((KVH, HEAD, WIDE), F32),
            pltpu.VMEM((ND, KVH, 2, TOK, HEAD), F32),
            pltpu.VMEM((ND, KVH, 2, TOK, HEAD), BF16),
            pltpu.VMEM((4, KVH, 2, TOK, HEAD), BF16),
            pltpu.VMEM((2, KVH, 2, TOK, HEAD), BF16),
            pltpu.VMEM((KVH, 2, TOK, HEAD), BF16),
            pltpu.VMEM((KVH, 2, TOK, HEAD), BF16),
            pltpu.SemaphoreType.DMA((4, 2)),
            pltpu.SemaphoreType.DMA((3, 6)),
            pltpu.SemaphoreType.DMA((3, 6)),
            pltpu.SemaphoreType.DMA((10, KVH)),
            pltpu.SemaphoreType.DMA((ND, KVH)),
            pltpu.SemaphoreType.DMA((8, KVH)),
            pltpu.SemaphoreType.DMA((8, KVH)),
        ],
        compiler_params=pltpu.CompilerParams(
            collective_id=0,
            has_side_effects=True,
            vmem_limit_bytes=60 * 1024 * 1024,
        ),
        cost_estimate=pl.CostEstimate(
            flops=8 * 10**9, bytes_accessed=3 * 10**6, transcendentals=5 * 10**6
        ),
    )(doc_ids, block_home, queries, key_states, value_vector_rows, grad_output)
    return out


def solution(mesh):
    return jax.shard_map(
        per_device,
        mesh=mesh,
        in_specs=(
            P(("seq", "head"), None),
            P(("seq", "head"), None),
            P(("seq", "head"), None),
            P(("seq", "head"), None),
            P(),
            P(),
        ),
        out_specs=(P("seq", "head"), P("seq", "head"), P("seq", "head"), P("seq", "head")),
        check_vma=False,
    )
```

```python
import math

import jax
import jax.numpy as jnp
from jax import lax
from jax.experimental import pallas as pl
from jax.experimental.pallas import tpu as pltpu
from jax.sharding import PartitionSpec as P

BLK = 128
HEAD = 128
TOK = 256
QH = 8
KVH = 2
PER = 4
QW = QH * HEAD
KW = KVH * HEAD
NSEQ = 128
ND = 9
WIDE = PER * TOK
SCALE = 1.0 / math.sqrt(HEAD)
C2 = SCALE * math.log2(math.e)
LOW = -1e30
ORDER = (0, 8, 4, 2, 1, 3, 6, 5, 7)
PLACE = {d: i for i, d in enumerate(ORDER)}
EARLY = 6
MESH = pl.DeviceIdType.MESH
F32 = jnp.float32
BF16 = jnp.bfloat16


def dot(a, b):
    return lax.dot_general(a, b, (((1,), (0,)), ((), ())), preferred_element_type=F32)


def dot_nt(a, b):
    return lax.dot_general(a, b, (((1,), (1,)), ((), ())), preferred_element_type=F32)


def flip(a):
    return jnp.transpose(a, (1, 0))


def kernel(
    doc_ref,
    home_ref,
    q_in,
    k_in,
    v_in,
    g_in,
    att_out,
    dq_out,
    dk_out,
    dv_out,
    att_ref,
    dq_ref,
    dk_ref,
    dv_ref,
    loc_q,
    loc_k,
    loc_v,
    loc_g,
    m_out,
    m_got,
    x_out,
    x_got,
    c_out,
    c_got,
    kv,
    kvt,
    qs,
    gs,
    gst,
    s_buf,
    p_buf,
    ds_buf,
    mx,
    peak,
    total,
    factor,
    delta,
    ot,
    attt,
    acc,
    sb,
    rr4,
    rr3,
    rr2,
    rr1,
    load_sem,
    out_sem,
    move_send,
    move_recv,
    halo_send,
    halo_recv,
    back_send,
    back_recv,
):
    s = lax.axis_index("seq")
    h = lax.axis_index("head")
    core = lax.rem(s, 2)
    xhi = lax.rem(lax.div(s, 2), 2)
    up4 = lax.rem(s + 4, NSEQ)
    down4 = lax.rem(s + NSEQ - 4, NSEQ)
    part_x = s + 2 - 4 * xhi
    part_c = s + 1 - 2 * core
    cross = jnp.clip(s - 1 + 2 * core, 0, NSEQ - 1)

    ins = (k_in, v_in, q_in, g_in)
    locs = (loc_k, loc_v, loc_q, loc_g)
    widths = (KW, KW, QW, QW)

    def load(a, half):
        return pltpu.make_async_copy(
            ins[a].at[:, pl.ds(half * widths[a], widths[a])],
            locs[a].at[half],
            load_sem.at[a, half],
        )

    for a in range(4):
        for half in range(2):
            load(a, half).start()

    barrier = pltpu.get_barrier_semaphore()

    def greet(seq, head):
        pl.semaphore_signal(barrier, inc=1, device_id=(seq, head), device_id_type=MESH)

    greet(s, 1 - h)
    greet(cross, 1 - h)
    for other in (part_c, part_x, up4, down4):
        greet(other, h)
    pl.semaphore_wait(barrier, 6)

    crosses = lax.div(home_ref[2 * s + h], 2) != part_c
    told = jnp.where(crosses, h, 1 - h)

    def column(i):
        if i < 2 * KVH:
            return i // KVH, i % KVH
        i -= 2 * KVH
        return 2 + i // QH, i % QH

    pieces = ((0, 1), (1, 2), (2, 3), (3, 4), (4, 8), (8, 12), (12, 16), (16, 20))
    chunks = range(2 * KVH)

    def own(i, half):
        a, c = column(i)
        return locs[a][half, :, pl.ds(c * HEAD, HEAD)]

    def move(way, piece):
        lo, hi = pieces[piece]
        src, dst, to = (
            (m_out, m_got, (s, 1 - h)),
            (x_out, x_got, (cross, 1 - h)),
            (c_out, c_got, (part_c, h)),
        )[way]
        return pltpu.make_async_remote_copy(
            src_ref=src.at[pl.ds(lo, hi - lo)],
            dst_ref=dst.at[pl.ds(lo, hi - lo)],
            send_sem=move_send.at[way, piece],
            recv_sem=move_recv.at[way, piece],
            device_id=to,
            device_id_type=MESH,
        )

    def tell(piece):
        for i in range(*pieces[piece]):
            m_out[i] = own(i, told)
        move(0, piece).start()

    def pass_on(piece):
        move(0, piece).wait_recv()
        for i in range(*pieces[piece]):
            got = m_got[i]
            x_out[i] = lax.select(crosses, own(i, 1 - h), got)
            c_out[i] = lax.select(crosses, got, own(i, h))
        move(1, piece).start()
        move(2, piece).start()

    inside = []
    for p in range(2):
        want = 2 * s + p
        inside.append((home_ref[2 * part_c] == want) | (home_ref[2 * part_c + 1] == want))

    def settle(piece):
        move(1, piece).wait_recv()
        move(2, piece).wait_recv()
        for i in range(*pieces[piece]):
            a, c = column(i)
            for p in range(2):
                block = lax.select(inside[p], c_got[i], x_got[i])
                if a < 2:
                    kv[0, c, a, pl.ds(p * BLK, BLK), :] = block
                else:
                    rows = pl.ds((c % PER) * TOK + p * BLK, BLK)
                    (qs if a == 2 else gs)[c // PER, rows, :] = block

    def halo(src, dst, seq, sem, i):
        g, kind = i % KVH, i // KVH
        return pltpu.make_async_remote_copy(
            src_ref=kv.at[src, g, kind],
            dst_ref=kv.at[dst, g, kind],
            send_sem=halo_send.at[sem, i],
            recv_sem=halo_recv.at[dst, i],
            device_id=(seq, h),
            device_id_type=MESH,
        )

    def have(d, i):
        ref = kv.at[d, i % KVH, i // KVH]
        pltpu.make_async_copy(ref, ref, halo_recv.at[d, i]).wait()

    z0, z4, z2, x0, x4, c0, c2, c4, c6, c8 = (
        [halo(src, dst, seq, sem, i) for i in chunks]
        for sem, (src, dst, seq) in enumerate(
            (
                (0, 4, up4),
                (4, 8, up4),
                (2, 6, up4),
                (0, 2, part_x),
                (4, 2, part_x),
                (0, 1, part_c),
                (2, 3 - 2 * core, part_c),
                (4, 5 - 2 * core, part_c),
                (6, 7 - 2 * core, part_c),
                (8, 7, part_c),
            )
        )
    )

    for a in (0, 1):
        for half in range(2):
            load(a, half).wait()
    for i in chunks:
        tell(i)
    acc[...] = jnp.zeros_like(acc)
    for i in chunks:
        pass_on(i)
    for a in (2, 3):
        for half in range(2):
            load(a, half).wait()
    tell(4)
    tell(5)
    mx[...] = jnp.full_like(mx, LOW)
    for i in chunks:
        settle(i)
        z0[i].start()

        @pl.when(xhi == 0)
        def _():
            x0[i].start()

        @pl.when(core == 0)
        def _():
            c0[i].start()

    def both(step):
        def body(g, carry):
            step(g)
            return carry

        lax.fori_loop(0, KVH, body, 0)

    def turn(d, g):
        cols = pl.ds(PLACE[d] * TOK, TOK)
        for kind in range(2):
            kvt[kind * KVH + g, :, cols] = flip(kv[d, g, kind])

    lane = lax.broadcasted_iota(jnp.int32, (1, TOK), 1)

    def hidden(d, pu):
        back = s - d
        key_doc = doc_ref[jnp.maximum(2 * back + pu, 0)]
        low = []
        for pt in range(2):
            seen = (doc_ref[2 * s + pt] == key_doc) & (back >= 0)
            low.append(jnp.where(seen, 0.0, LOW).astype(F32))
        return jnp.where(lane < BLK, low[0], low[1])

    def held(d):
        i = PLACE[d]
        return (i if i < EARLY else i - EARLY) * TOK

    def score(d, g):
        for j in range(PER):
            cols = pl.ds(j * TOK, TOK)
            tile = dot_nt(kv[d, g, 0], qs[g, cols, :])
            if d in (0, ND - 1):
                row = lax.broadcasted_iota(jnp.int32, (TOK, TOK), 0)
                col = lax.broadcasted_iota(jnp.int32, (TOK, TOK), 1)
                keep = row <= col if d == 0 else row > col
                tile = jnp.where(keep, tile, LOW)
            s_buf[g, pl.ds(held(d), TOK), cols] = tile
            best = mx[g, :, cols]
            for pu in range(2):
                top = jnp.max(tile[pu * BLK : (pu + 1) * BLK].reshape(BLK // 8, 8, TOK), axis=0)
                best = jnp.maximum(best, top + hidden(d, pu))
            mx[g, :, cols] = best

    def weigh(part, g):
        group = ORDER[:EARLY] if part == 0 else ORDER[EARLY:]
        first = 0 if part == 0 else EARLY * TOK
        for j in range(PER):
            cols = pl.ds(j * TOK, TOK)
            top = jnp.max(mx[g, :, cols], axis=0, keepdims=True) * C2
            peak[part, g, :, cols] = top
            added = jnp.zeros((8, TOK), F32)
            for d in group:
                for pu in range(2):
                    base = top - hidden(d, pu)
                    e = jnp.exp2(s_buf[g, pl.ds(held(d) + pu * BLK, BLK), cols] * C2 - base)
                    added = added + jnp.sum(e.reshape(BLK // 8, 8, TOK), axis=0)
                    p_buf[g, pl.ds(PLACE[d] * TOK + pu * BLK, BLK), cols] = e.astype(BF16)
            total[part, g, :, cols] = jnp.sum(added, axis=0, keepdims=True)
            rows = pl.ds(first, len(group) * TOK)
            ot[part, g, :, cols] = dot(kvt[KVH + g, :, rows], p_buf[g, rows, cols])

    def join(g):
        shift = jnp.exp2(peak[0, g] - peak[1, g])
        inv = 1.0 / (total[0, g] * shift + total[1, g])
        factor[0, g] = shift * inv
        factor[1, g] = inv
        a = (ot[0, g] * factor[0, g] + ot[1, g] * inv).astype(BF16)
        attt[g] = a
        for j in range(PER):
            cols = slice(j * TOK, (j + 1) * TOK)
            delta[g, :, cols] = jnp.sum(
                gst[g, :, cols].astype(F32) * a[:, cols].astype(F32), axis=0, keepdims=True
            )

    tell(6)
    tell(7)
    pass_on(4)
    pass_on(5)
    for i in chunks:
        have(4, i)
        z4[i].start()

        @pl.when(xhi == 1)
        def _():
            x4[i].start()

        c4[i].start()
    both(lambda g: turn(0, g))
    both(lambda g: turn(4, g))
    settle(4)
    settle(5)
    both(lambda g: score(0, g))
    both(lambda g: score(4, g))
    for i in chunks:
        have(2, i)
        z2[i].start()
        c2[i].start()
    pass_on(6)
    pass_on(7)
    both(lambda g: turn(2, g))
    both(lambda g: score(2, g))
    for i in chunks:
        have(8, i)

        @pl.when(core == 1)
        def _():
            c8[i].start()

    for d in (8, 1, 3):
        if d < 8:
            for i in chunks:
                have(d, i)
        both(lambda g: turn(d, g))
        both(lambda g: score(d, g))
    weigh(0, 0)
    for i in chunks:
        have(6, i)
        c6[i].start()
    weigh(0, 1)
    both(lambda g: turn(6, g))
    both(lambda g: score(6, g))
    for d in (5, 7):
        for i in chunks:
            have(d, i)
        both(lambda g: turn(d, g))
        both(lambda g: score(d, g))
    settle(6)
    settle(7)

    def finish(g):
        for j in range(PER):
            cols = pl.ds(j * TOK, TOK)
            gst[g, :, cols] = flip(gs[g, cols, :])
        weigh(1, g)
        join(g)

    both(finish)

    def slope(d, g):
        rows = pl.ds(PLACE[d] * TOK, TOK)
        part = 0 if PLACE[d] < EARLY else 1
        for j in range(PER):
            cols = pl.ds(j * TOK, TOK)
            dp = dot(kv[d, g, 1], gst[g, :, cols])
            prob = p_buf[g, rows, cols].astype(F32) * factor[part, g, :, cols]
            p_buf[g, rows, cols] = prob.astype(BF16)
            ds_buf[g, rows, cols] = (prob * (dp - delta[g, :, cols])).astype(BF16)
        acc[d, g, 0] += dot(ds_buf[g, rows, :], qs[g])
        acc[d, g, 1] += dot(p_buf[g, rows, :], gs[g])

    def give(d, dst, seq, sem):
        return [
            pltpu.make_async_remote_copy(
                src_ref=sb.at[d, i % KVH, i // KVH],
                dst_ref=dst.at[i % KVH, i // KVH],
                send_sem=back_send.at[sem, i],
                recv_sem=back_recv.at[sem, i],
                device_id=(seq, h),
                device_id_type=MESH,
            )
            for i in chunks
        ]

    b7 = give(7, rr4.at[3], part_c, 3)
    b5 = give(5, rr4.at[2], part_c, 2)
    b3 = give(3, rr4.at[1], part_c, 1)
    b1 = give(1, rr4.at[0], part_c, 0)
    b6 = give(6, rr3.at[1], down4, 5)
    b2 = give(2, rr3.at[0], part_x, 4)
    b8 = give(8, rr2, down4, 6)
    b4 = give(4, rr1, down4, 7)

    def post(d, copy, i):
        sb[d, i % KVH, i // KVH] = acc[d, i % KVH, i // KVH].astype(BF16)
        copy[i].start()

    def take(copy, ref, d, i):
        copy[i].wait_recv()
        acc[d, i % KVH, i // KVH] += ref[i % KVH, i // KVH].astype(F32)

    def leave(i, ref, out):
        return pltpu.make_async_copy(ref, out, out_sem.at[i])

    outs = [
        leave(i, *pair)
        for i, pair in enumerate(
            ((att_ref, att_out), (dq_ref, dq_out), (dk_ref, dk_out), (dv_ref, dv_out))
        )
    ]

    def kinds(g):
        return (g, g + KVH)

    for d, copy in ((7, b7), (5, b5)):
        for g in range(KVH):
            slope(d, g)
            for i in kinds(g):
                post(d, copy, i)
    for g in range(KVH):
        slope(6, g)
        for i in kinds(g):
            take(b7, rr4.at[3], 6 + 2 * core, i)
            take(b5, rr4.at[2], 4 + 2 * core, i)
            post(6, b6, i)
    for g in range(KVH):
        slope(8, g)
        for i in kinds(g):
            post(8, b8, i)
    for d, copy in ((3, b3), (1, b1)):
        for g in range(KVH):
            slope(d, g)
            for i in kinds(g):
                post(d, copy, i)
    for g in range(KVH):
        slope(2, g)
        for i in kinds(g):
            take(b3, rr4.at[1], 2 + 2 * core, i)
            take(b1, rr4.at[0], 2 * core, i)
            take(b6, rr3.at[1], 2, i)
            post(2, b2, i)
    for g in range(KVH):
        slope(4, g)
        slope(0, g)
    for i in range(QH):
        g, j = i // PER, i % PER
        cols = pl.ds(j * TOK, TOK)
        att_ref[:, pl.ds(i * HEAD, HEAD)] = flip(attt[g, :, cols])
    outs[0].start()
    for i in range(QH):
        g, j = i // PER, i % PER
        term = dot(kvt[g], ds_buf[g, :, pl.ds(j * TOK, TOK)])
        dq_ref[:, pl.ds(i * HEAD, HEAD)] = flip((term * SCALE).astype(BF16))
    outs[1].start()
    for g in range(KVH):
        for i in kinds(g):
            take(b8, rr2, 4, i)
            take(b2, rr3.at[0], 4 * xhi, i)
            post(4, b4, i)
    for g in range(KVH):
        for i in kinds(g):
            take(b4, rr1, 0, i)
        dk_ref[:, pl.ds(g * HEAD, HEAD)] = (acc[0, g, 0] * SCALE).astype(BF16)
        dv_ref[:, pl.ds(g * HEAD, HEAD)] = acc[0, g, 1].astype(BF16)
    outs[2].start()
    outs[3].start()

    for way in range(3):
        for piece in range(len(pieces)):
            move(way, piece).wait_send()
    for copy in (z0, z4, z2, c2, c4, c6, b7, b5, b3, b1, b6, b2, b8, b4):
        for i in chunks:
            copy[i].wait_send()

    for ahead, copy in ((xhi == 0, x0), (xhi == 1, x4), (core == 0, c0), (core == 1, c8)):

        @pl.when(ahead)
        def _():
            for i in chunks:
                copy[i].wait_send()

    for copy in outs:
        copy.wait()


def place_kernel(*refs):
    ins, outs, held, sem = refs[:4], refs[4:8], refs[8:12], refs[12]
    reads = [pltpu.make_async_copy(ins[i], held[i], sem.at[0, i]) for i in range(4)]
    writes = [pltpu.make_async_copy(held[i], outs[i], sem.at[1, i]) for i in range(4)]
    for copy in reads:
        copy.start()
    for read, write in zip(reads, writes):
        read.wait()
        write.start()
    for copy in writes:
        copy.wait()


def per_device(queries, key_states, value_vector_rows, grad_output, doc_ids, block_home):
    smem = pl.BlockSpec(memory_space=pltpu.SMEM)
    anywhere = pl.BlockSpec(memory_space=pl.ANY)
    shapes = (
        jax.ShapeDtypeStruct((TOK, QW), BF16),
        jax.ShapeDtypeStruct((TOK, QW), BF16),
        jax.ShapeDtypeStruct((TOK, KW), BF16),
        jax.ShapeDtypeStruct((TOK, KW), BF16),
    )
    out = pl.pallas_call(
        kernel,
        out_shape=shapes,
        in_specs=[smem, smem, anywhere, anywhere, anywhere, anywhere],
        out_specs=(anywhere, anywhere, anywhere, anywhere),
        scratch_shapes=[
            *[pltpu.VMEM(shape.shape, BF16) for shape in shapes],
            pltpu.VMEM((2, BLK, QW), BF16),
            pltpu.VMEM((2, BLK, KW), BF16),
            pltpu.VMEM((2, BLK, KW), BF16),
            pltpu.VMEM((2, BLK, QW), BF16),
            *[pltpu.VMEM((2 * KVH + 2 * QH, BLK, HEAD), BF16) for _ in range(6)],
            pltpu.VMEM((ND, KVH, 2, TOK, HEAD), BF16),
            pltpu.VMEM((2 * KVH, HEAD, ND * TOK), BF16),
            pltpu.VMEM((KVH, WIDE, HEAD), BF16),
            pltpu.VMEM((KVH, WIDE, HEAD), BF16),
            pltpu.VMEM((KVH, HEAD, WIDE), BF16),
            pltpu.VMEM((KVH, EARLY * TOK, WIDE), F32),
            pltpu.VMEM((KVH, ND * TOK, WIDE), BF16),
            pltpu.VMEM((KVH, ND * TOK, WIDE), BF16),
            pltpu.VMEM((KVH, 8, WIDE), F32),
            pltpu.VMEM((2, KVH, 1, WIDE), F32),
            pltpu.VMEM((2, KVH, 1, WIDE), F32),
            pltpu.VMEM((2, KVH, 1, WIDE), F32),
            pltpu.VMEM((KVH, 1, WIDE), F32),
            pltpu.VMEM((2, KVH, HEAD, WIDE), F32),
            pltpu.VMEM((KVH, HEAD, WIDE), BF16),
            pltpu.VMEM((ND, KVH, 2, TOK, HEAD), F32),
            pltpu.VMEM((ND, KVH, 2, TOK, HEAD), BF16),
            pltpu.VMEM((4, KVH, 2, TOK, HEAD), BF16),
            pltpu.VMEM((2, KVH, 2, TOK, HEAD), BF16),
            pltpu.VMEM((KVH, 2, TOK, HEAD), BF16),
            pltpu.VMEM((KVH, 2, TOK, HEAD), BF16),
            pltpu.SemaphoreType.DMA((4, 2)),
            pltpu.SemaphoreType.DMA((4,)),
            pltpu.SemaphoreType.DMA((3, 8)),
            pltpu.SemaphoreType.DMA((3, 8)),
            pltpu.SemaphoreType.DMA((10, 2 * KVH)),
            pltpu.SemaphoreType.DMA((ND, 2 * KVH)),
            pltpu.SemaphoreType.DMA((8, 2 * KVH)),
            pltpu.SemaphoreType.DMA((8, 2 * KVH)),
        ],
        compiler_params=pltpu.CompilerParams(
            collective_id=0,
            has_side_effects=True,
            vmem_limit_bytes=60 * 1024 * 1024,
        ),
        cost_estimate=pl.CostEstimate(
            flops=8 * 10**9, bytes_accessed=3 * 10**6, transcendentals=5 * 10**6
        ),
    )(doc_ids, block_home, queries, key_states, value_vector_rows, grad_output)
    return pl.pallas_call(
        place_kernel,
        out_shape=shapes,
        in_specs=[anywhere] * 4,
        out_specs=(anywhere,) * 4,
        scratch_shapes=[
            *[pltpu.VMEM(shape.shape, BF16) for shape in shapes],
            pltpu.SemaphoreType.DMA((2, 4)),
        ],
    )(*out)


def solution(mesh):
    return jax.shard_map(
        per_device,
        mesh=mesh,
        in_specs=(
            P(("seq", "head"), None),
            P(("seq", "head"), None),
            P(("seq", "head"), None),
            P(("seq", "head"), None),
            P(),
            P(),
        ),
        out_specs=(P("seq", "head"), P("seq", "head"), P("seq", "head"), P("seq", "head")),
        check_vma=False,
    )
```

```python
import math

import jax
import jax.numpy as jnp
from jax import lax
from jax.experimental import pallas as pl
from jax.experimental.pallas import tpu as pltpu
from jax.sharding import PartitionSpec as P

BLK = 128
HEAD = 128
TOK = 256
QH = 8
KVH = 2
PER = 4
QW = QH * HEAD
KW = KVH * HEAD
NSEQ = 128
ND = 9
WIDE = PER * TOK
SCALE = 1.0 / math.sqrt(HEAD)
C2 = SCALE * math.log2(math.e)
LOW = -1e30
ORDER = (0, 8, 4, 2, 1, 3, 6, 5, 7)
PLACE = {d: i for i, d in enumerate(ORDER)}
EARLY = 6
MESH = pl.DeviceIdType.MESH
F32 = jnp.float32
BF16 = jnp.bfloat16


def dot(a, b):
    return lax.dot_general(a, b, (((1,), (0,)), ((), ())), preferred_element_type=F32)


def dot_nt(a, b):
    return lax.dot_general(a, b, (((1,), (1,)), ((), ())), preferred_element_type=F32)


def flip(a):
    return jnp.transpose(a, (1, 0))


def kernel(
    doc_ref,
    home_ref,
    q_in,
    k_in,
    v_in,
    g_in,
    att_out,
    dq_out,
    dk_out,
    dv_out,
    att_ref,
    dq_ref,
    dk_ref,
    dv_ref,
    loc_q,
    loc_k,
    loc_v,
    loc_g,
    m_out,
    m_got,
    x_out,
    x_got,
    c_out,
    c_got,
    kv,
    kvt,
    qs,
    gs,
    gst,
    s_buf,
    p_buf,
    ds_buf,
    mx,
    peak,
    total,
    factor,
    delta,
    ot,
    attt,
    acc,
    sb,
    rr4,
    rr3,
    rr2,
    rr1,
    load_sem,
    out_sem,
    move_send,
    move_recv,
    halo_send,
    halo_recv,
    back_send,
    back_recv,
):
    s = lax.axis_index("seq")
    h = lax.axis_index("head")
    core = lax.rem(s, 2)
    xhi = lax.rem(lax.div(s, 2), 2)
    up4 = lax.rem(s + 4, NSEQ)
    down4 = lax.rem(s + NSEQ - 4, NSEQ)
    part_x = s + 2 - 4 * xhi
    part_c = s + 1 - 2 * core
    cross = jnp.clip(s - 1 + 2 * core, 0, NSEQ - 1)

    ins = (k_in, v_in, q_in, g_in)
    locs = (loc_k, loc_v, loc_q, loc_g)
    widths = (KW, KW, QW, QW)

    def load(a, half):
        return pltpu.make_async_copy(
            ins[a].at[:, pl.ds(half * widths[a], widths[a])],
            locs[a].at[half],
            load_sem.at[a, half],
        )

    for a in range(4):
        for half in range(2):
            load(a, half).start()

    barrier = pltpu.get_barrier_semaphore()

    def greet(seq, head):
        pl.semaphore_signal(barrier, inc=1, device_id=(seq, head), device_id_type=MESH)

    greet(s, 1 - h)
    greet(cross, 1 - h)
    for other in (part_c, part_x, up4, down4):
        greet(other, h)
    pl.semaphore_wait(barrier, 6)

    crosses = lax.div(home_ref[2 * s + h], 2) != part_c
    told = jnp.where(crosses, h, 1 - h)

    def column(i):
        if i < 2 * KVH:
            return i // KVH, i % KVH
        i -= 2 * KVH
        return 2 + i // QH, i % QH

    pieces = ((0, 1), (1, 2), (2, 3), (3, 4), (4, 8), (8, 12), (12, 16), (16, 20))
    chunks = range(2 * KVH)
    by_z = (0, KVH)

    def own(i, half):
        a, c = column(i)
        return locs[a][half, :, pl.ds(c * HEAD, HEAD)]

    def move(way, piece):
        lo, hi = pieces[piece]
        src, dst, to = (
            (m_out, m_got, (s, 1 - h)),
            (x_out, x_got, (cross, 1 - h)),
            (c_out, c_got, (part_c, h)),
        )[way]
        return pltpu.make_async_remote_copy(
            src_ref=src.at[pl.ds(lo, hi - lo)],
            dst_ref=dst.at[pl.ds(lo, hi - lo)],
            send_sem=move_send.at[way, piece],
            recv_sem=move_recv.at[way, piece],
            device_id=to,
            device_id_type=MESH,
        )

    def tell(piece):
        for i in range(*pieces[piece]):
            m_out[i] = own(i, told)
        move(0, piece).start()

    def pass_on(piece):
        move(0, piece).wait_recv()
        for i in range(*pieces[piece]):
            got = m_got[i]
            x_out[i] = lax.select(crosses, own(i, 1 - h), got)
            c_out[i] = lax.select(crosses, got, own(i, h))
        move(1, piece).start()
        move(2, piece).start()

    inside = []
    for p in range(2):
        want = 2 * s + p
        inside.append((home_ref[2 * part_c] == want) | (home_ref[2 * part_c + 1] == want))

    def settle(piece):
        move(1, piece).wait_recv()
        move(2, piece).wait_recv()
        for i in range(*pieces[piece]):
            a, c = column(i)
            for p in range(2):
                block = lax.select(inside[p], c_got[i], x_got[i])
                if a < 2:
                    kv[0, c, a, pl.ds(p * BLK, BLK), :] = block
                else:
                    rows = pl.ds((c % PER) * TOK + p * BLK, BLK)
                    (qs if a == 2 else gs)[c // PER, rows, :] = block

    def halo(src, dst, seq, sem, i):
        g, kind = i % KVH, i // KVH
        return pltpu.make_async_remote_copy(
            src_ref=kv.at[src, g, kind],
            dst_ref=kv.at[dst, g, kind],
            send_sem=halo_send.at[sem, i],
            recv_sem=halo_recv.at[dst, i],
            device_id=(seq, h),
            device_id_type=MESH,
        )

    def have(d, i):
        ref = kv.at[d, i % KVH, i // KVH]
        pltpu.make_async_copy(ref, ref, halo_recv.at[d, i]).wait()

    z0, z4, z2, x0, x4, c0, c2, c4, c6, c8 = (
        [halo(src, dst, seq, sem, i) for i in chunks]
        for sem, (src, dst, seq) in enumerate(
            (
                (0, 4, up4),
                (4, 8, up4),
                (2, 6, up4),
                (0, 2, part_x),
                (4, 2, part_x),
                (0, 1, part_c),
                (2, 3 - 2 * core, part_c),
                (4, 5 - 2 * core, part_c),
                (6, 7 - 2 * core, part_c),
                (8, 7, part_c),
            )
        )
    )

    for a in (0, 1):
        for half in range(2):
            load(a, half).wait()
    for i in chunks:
        tell(i)
    acc[...] = jnp.zeros_like(acc)
    for i in chunks:
        pass_on(i)
    for a in (2, 3):
        for half in range(2):
            load(a, half).wait()
    tell(4)
    tell(5)
    mx[...] = jnp.full_like(mx, LOW)
    for i in chunks:
        settle(i)
        z0[i].start()

        @pl.when(xhi == 0)
        def _():
            x0[i].start()

        @pl.when(core == 0)
        def _():
            c0[i].start()

    def both(step):
        def body(g, carry):
            step(g)
            return carry

        lax.fori_loop(0, KVH, body, 0)

    def turn(d, g):
        kvt[KVH + g, :, pl.ds(PLACE[d] * TOK, TOK)] = flip(kv[d, g, 1])

    def turn_key(d, g):
        kvt[g, :, pl.ds(PLACE[d] * TOK, TOK)] = flip(kv[d, g, 0])

    lane = lax.broadcasted_iota(jnp.int32, (1, TOK), 1)

    def hidden(d, pu):
        back = s - d
        key_doc = doc_ref[jnp.maximum(2 * back + pu, 0)]
        low = []
        for pt in range(2):
            seen = (doc_ref[2 * s + pt] == key_doc) & (back >= 0)
            low.append(jnp.where(seen, 0.0, LOW).astype(F32))
        return jnp.where(lane < BLK, low[0], low[1])

    def held(d):
        i = PLACE[d]
        return (i if i < EARLY else i - EARLY) * TOK

    def score(d, g):
        for j in range(PER):
            cols = pl.ds(j * TOK, TOK)
            tile = dot_nt(kv[d, g, 0], qs[g, cols, :])
            if d in (0, ND - 1):
                row = lax.broadcasted_iota(jnp.int32, (TOK, TOK), 0)
                col = lax.broadcasted_iota(jnp.int32, (TOK, TOK), 1)
                keep = row <= col if d == 0 else row > col
                tile = jnp.where(keep, tile, LOW)
            s_buf[g, pl.ds(held(d), TOK), cols] = tile
            best = mx[g, :, cols]
            for pu in range(2):
                top = jnp.max(tile[pu * BLK : (pu + 1) * BLK].reshape(BLK // 8, 8, TOK), axis=0)
                best = jnp.maximum(best, top + hidden(d, pu))
            mx[g, :, cols] = best

    def weigh(part, g):
        group = ORDER[:EARLY] if part == 0 else ORDER[EARLY:]
        first = 0 if part == 0 else EARLY * TOK
        for j in range(PER):
            cols = pl.ds(j * TOK, TOK)
            top = jnp.max(mx[g, :, cols], axis=0, keepdims=True) * C2
            peak[part, g, :, cols] = top
            added = jnp.zeros((8, TOK), F32)
            for d in group:
                for pu in range(2):
                    base = top - hidden(d, pu)
                    e = jnp.exp2(s_buf[g, pl.ds(held(d) + pu * BLK, BLK), cols] * C2 - base)
                    added = added + jnp.sum(e.reshape(BLK // 8, 8, TOK), axis=0)
                    p_buf[g, pl.ds(PLACE[d] * TOK + pu * BLK, BLK), cols] = e.astype(BF16)
            total[part, g, :, cols] = jnp.sum(added, axis=0, keepdims=True)
            rows = pl.ds(first, len(group) * TOK)
            ot[part, g, :, cols] = dot(kvt[KVH + g, :, rows], p_buf[g, rows, cols])

    def join(g):
        shift = jnp.exp2(peak[0, g] - peak[1, g])
        inv = 1.0 / (total[0, g] * shift + total[1, g])
        factor[0, g] = shift * inv
        factor[1, g] = inv
        a = (ot[0, g] * factor[0, g] + ot[1, g] * inv).astype(BF16)
        attt[g] = a
        for j in range(PER):
            cols = slice(j * TOK, (j + 1) * TOK)
            delta[g, :, cols] = jnp.sum(
                gst[g, :, cols].astype(F32) * a[:, cols].astype(F32), axis=0, keepdims=True
            )

    pass_on(4)
    pass_on(5)
    for i in chunks:
        have(4, i)
        z4[i].start()

        @pl.when(xhi == 1)
        def _():
            x4[i].start()

        c4[i].start()
    tell(6)
    tell(7)
    both(lambda g: turn(0, g))
    both(lambda g: turn(4, g))
    settle(4)
    settle(5)
    both(lambda g: score(0, g))
    both(lambda g: score(4, g))
    for i in chunks:
        have(2, i)
        z2[i].start()
        c2[i].start()
    pass_on(6)
    pass_on(7)
    both(lambda g: turn(2, g))
    both(lambda g: score(2, g))
    for i in chunks:
        have(8, i)
        @pl.when(core == 1)
        def _():
            c8[i].start()

    for d in (8, 1, 3):
        if d < 8:
            for i in chunks:
                have(d, i)
        both(lambda g: turn(d, g))
        both(lambda g: score(d, g))
    weigh(0, 0)
    for i in chunks:
        have(6, i)
        c6[i].start()
    weigh(0, 1)
    both(lambda g: turn(6, g))
    both(lambda g: score(6, g))
    for d in (5, 7):
        for i in chunks:
            have(d, i)
        both(lambda g: turn(d, g))
        both(lambda g: score(d, g))
    settle(6)
    settle(7)

    def finish(g):
        for j in range(PER):
            cols = pl.ds(j * TOK, TOK)
            gst[g, :, cols] = flip(gs[g, cols, :])
        weigh(1, g)
        join(g)

    def slope(d, g):
        rows = pl.ds(PLACE[d] * TOK, TOK)
        part = 0 if PLACE[d] < EARLY else 1
        for j in range(PER):
            cols = pl.ds(j * TOK, TOK)
            dp = dot(kv[d, g, 1], gst[g, :, cols])
            prob = p_buf[g, rows, cols].astype(F32) * factor[part, g, :, cols]
            p_buf[g, rows, cols] = prob.astype(BF16)
            ds_buf[g, rows, cols] = (prob * (dp - delta[g, :, cols])).astype(BF16)
        acc[d, g, 0] += dot(ds_buf[g, rows, :], qs[g])
        acc[d, g, 1] += dot(p_buf[g, rows, :], gs[g])

    def give(d, dst, seq, seq_x, sem):
        return [
            pltpu.make_async_remote_copy(
                src_ref=sb.at[d, i % KVH, i // KVH],
                dst_ref=dst.at[i % KVH, i // KVH],
                send_sem=back_send.at[sem, i],
                recv_sem=back_recv.at[sem, i],
                device_id=(seq if i in by_z else seq_x, h),
                device_id_type=MESH,
            )
            for i in chunks
        ]

    b7 = give(7, rr4.at[3], part_c, part_c, 3)
    b5 = give(5, rr4.at[2], part_c, part_c, 2)
    b3 = give(3, rr4.at[1], part_c, part_c, 1)
    b1 = give(1, rr4.at[0], part_c, part_c, 0)
    b6 = give(6, rr3.at[1], down4, part_x, 5)
    b2 = give(2, rr3.at[0], part_x, part_x, 4)
    b8 = give(8, rr2, down4, down4, 6)
    b4 = give(4, rr1, down4, down4, 7)

    def post(d, copy, i):
        sb[d, i % KVH, i // KVH] = acc[d, i % KVH, i // KVH].astype(BF16)
        copy[i].start()

    def take(copy, ref, d, i):
        copy[i].wait_recv()
        acc[d, i % KVH, i // KVH] += ref[i % KVH, i // KVH].astype(F32)

    def leave(i, ref, out):
        return pltpu.make_async_copy(ref, out, out_sem.at[i])

    outs = [
        leave(i, *pair)
        for i, pair in enumerate(
            ((att_ref, att_out), (dq_ref, dq_out), (dk_ref, dk_out), (dv_ref, dv_out))
        )
    ]

    def kinds(g):
        return (g, g + KVH)

    def near(d, copy, g):
        slope(d, g)
        for i in kinds(g):
            post(d, copy, i)

    def sixth(g):
        slope(6, g)
        for i in kinds(g):
            take(b7, rr4.at[3], 6 + 2 * core, i)
            take(b5, rr4.at[2], 4 + 2 * core, i)
            post(6, b6, i)

    finish(0)
    near(7, b7, 0)
    near(5, b5, 0)
    finish(1)
    near(7, b7, 1)
    near(5, b5, 1)
    sixth(0)
    near(8, b8, 0)
    near(3, b3, 0)
    near(1, b1, 0)
    sixth(1)
    near(3, b3, 1)
    near(1, b1, 1)
    slope(2, 0)
    slope(8, 1)
    slope(2, 1)
    slope(4, 0)
    for i in kinds(0):
        take(b3, rr4.at[1], 2 + 2 * core, i)
        take(b1, rr4.at[0], 2 * core, i)
        take(b6, rr3.at[1], 2, i)
        post(2, b2, i)
    slope(4, 1)
    for i in kinds(1):
        take(b3, rr4.at[1], 2 + 2 * core, i)
        take(b1, rr4.at[0], 2 * core, i)
        take(b6, rr3.at[1], 4 + 4 * xhi, i)
        post(8, b8, i)
        post(2, b2, i)
    slope(0, 0)
    slope(0, 1)
    for d in ORDER:
        both(lambda g: turn_key(d, g))
    for i in range(QH):
        g, j = i // PER, i % PER
        cols = pl.ds(j * TOK, TOK)
        att_ref[:, pl.ds(i * HEAD, HEAD)] = flip(attt[g, :, cols])
    outs[0].start()
    for i in range(QH):
        g, j = i // PER, i % PER
        term = dot(kvt[g], ds_buf[g, :, pl.ds(j * TOK, TOK)])
        dq_ref[:, pl.ds(i * HEAD, HEAD)] = flip((term * SCALE).astype(BF16))
    outs[1].start()
    for g in range(KVH):
        for i in kinds(g):
            take(b8, rr2, 4, i)
            take(b2, rr3.at[0], 4 * xhi, i)
            post(4, b4, i)
    for g in range(KVH):
        for i in kinds(g):
            take(b4, rr1, 0, i)
        dk_ref[:, pl.ds(g * HEAD, HEAD)] = (acc[0, g, 0] * SCALE).astype(BF16)
        dv_ref[:, pl.ds(g * HEAD, HEAD)] = acc[0, g, 1].astype(BF16)
    outs[2].start()
    outs[3].start()

    for way in range(3):
        for piece in range(len(pieces)):
            move(way, piece).wait_send()
    for copy in (z0, z4, z2, c2, c4, c6, b7, b5, b3, b1, b6, b2, b8, b4):
        for i in chunks:
            copy[i].wait_send()

    for ahead, copy in ((xhi == 0, x0), (xhi == 1, x4), (core == 0, c0), (core == 1, c8)):

        @pl.when(ahead)
        def _():
            for i in chunks:
                copy[i].wait_send()

    for copy in outs:
        copy.wait()


def place_kernel(*refs):
    ins, outs, held, sem = refs[:4], refs[4:8], refs[8:12], refs[12]
    reads = [pltpu.make_async_copy(ins[i], held[i], sem.at[0, i]) for i in range(4)]
    writes = [pltpu.make_async_copy(held[i], outs[i], sem.at[1, i]) for i in range(4)]
    for copy in reads:
        copy.start()
    for read, write in zip(reads, writes):
        read.wait()
        write.start()
    for copy in writes:
        copy.wait()


def per_device(queries, key_states, value_vector_rows, grad_output, doc_ids, block_home):
    smem = pl.BlockSpec(memory_space=pltpu.SMEM)
    anywhere = pl.BlockSpec(memory_space=pl.ANY)
    shapes = (
        jax.ShapeDtypeStruct((TOK, QW), BF16),
        jax.ShapeDtypeStruct((TOK, QW), BF16),
        jax.ShapeDtypeStruct((TOK, KW), BF16),
        jax.ShapeDtypeStruct((TOK, KW), BF16),
    )
    out = pl.pallas_call(
        kernel,
        out_shape=shapes,
        in_specs=[smem, smem, anywhere, anywhere, anywhere, anywhere],
        out_specs=(anywhere, anywhere, anywhere, anywhere),
        scratch_shapes=[
            *[pltpu.VMEM(shape.shape, BF16) for shape in shapes],
            pltpu.VMEM((2, BLK, QW), BF16),
            pltpu.VMEM((2, BLK, KW), BF16),
            pltpu.VMEM((2, BLK, KW), BF16),
            pltpu.VMEM((2, BLK, QW), BF16),
            *[pltpu.VMEM((2 * KVH + 2 * QH, BLK, HEAD), BF16) for _ in range(6)],
            pltpu.VMEM((ND, KVH, 2, TOK, HEAD), BF16),
            pltpu.VMEM((2 * KVH, HEAD, ND * TOK), BF16),
            pltpu.VMEM((KVH, WIDE, HEAD), BF16),
            pltpu.VMEM((KVH, WIDE, HEAD), BF16),
            pltpu.VMEM((KVH, HEAD, WIDE), BF16),
            pltpu.VMEM((KVH, EARLY * TOK, WIDE), F32),
            pltpu.VMEM((KVH, ND * TOK, WIDE), BF16),
            pltpu.VMEM((KVH, ND * TOK, WIDE), BF16),
            pltpu.VMEM((KVH, 8, WIDE), F32),
            pltpu.VMEM((2, KVH, 1, WIDE), F32),
            pltpu.VMEM((2, KVH, 1, WIDE), F32),
            pltpu.VMEM((2, KVH, 1, WIDE), F32),
            pltpu.VMEM((KVH, 1, WIDE), F32),
            pltpu.VMEM((2, KVH, HEAD, WIDE), F32),
            pltpu.VMEM((KVH, HEAD, WIDE), BF16),
            pltpu.VMEM((ND, KVH, 2, TOK, HEAD), F32),
            pltpu.VMEM((ND, KVH, 2, TOK, HEAD), BF16),
            pltpu.VMEM((4, KVH, 2, TOK, HEAD), BF16),
            pltpu.VMEM((2, KVH, 2, TOK, HEAD), BF16),
            pltpu.VMEM((KVH, 2, TOK, HEAD), BF16),
            pltpu.VMEM((KVH, 2, TOK, HEAD), BF16),
            pltpu.SemaphoreType.DMA((4, 2)),
            pltpu.SemaphoreType.DMA((4,)),
            pltpu.SemaphoreType.DMA((3, 8)),
            pltpu.SemaphoreType.DMA((3, 8)),
            pltpu.SemaphoreType.DMA((10, 2 * KVH)),
            pltpu.SemaphoreType.DMA((ND, 2 * KVH)),
            pltpu.SemaphoreType.DMA((8, 2 * KVH)),
            pltpu.SemaphoreType.DMA((8, 2 * KVH)),
        ],
        compiler_params=pltpu.CompilerParams(
            collective_id=0,
            has_side_effects=True,
            vmem_limit_bytes=60 * 1024 * 1024,
        ),
        cost_estimate=pl.CostEstimate(
            flops=8 * 10**9, bytes_accessed=3 * 10**6, transcendentals=5 * 10**6
        ),
    )(doc_ids, block_home, queries, key_states, value_vector_rows, grad_output)
    return pl.pallas_call(
        place_kernel,
        out_shape=shapes,
        in_specs=[anywhere] * 4,
        out_specs=(anywhere,) * 4,
        scratch_shapes=[
            *[pltpu.VMEM(shape.shape, BF16) for shape in shapes],
            pltpu.SemaphoreType.DMA((2, 4)),
        ],
    )(*out)


def solution(mesh):
    return jax.shard_map(
        per_device,
        mesh=mesh,
        in_specs=(
            P(("seq", "head"), None),
            P(("seq", "head"), None),
            P(("seq", "head"), None),
            P(("seq", "head"), None),
            P(),
            P(),
        ),
        out_specs=(P("seq", "head"), P("seq", "head"), P("seq", "head"), P("seq", "head")),
        check_vma=False,
    )
```
